256 devices in a mesh: row: 32 (over y, z), col: 8 (over x, core).
Axes of the slice: x: 4, y: 4, z: 8, core: 2. Of those that a mesh axis runs over, the one named last changes fastest.
Arguments:
- matrix: float32 [16384, 16384], P('row', 'col'), may hold values from -9 to 9
- reflectors: float32 [16384, 512], P('row'), may hold values from -4 to 4
Outputs:
- banded: float32 [16384, 16384], P('row', 'col')
The draws below stay inside these ranges and needn't reach their ends.
All inputs are finite; a program needn't handle non-finite values.
Results may differ from the reference program's by a relative error of at most 0.0001.
Values sent between devices are 32-bit elements; how exact they have to be, the bound alone decides.
No kernel may reach another device: no remote copies, remote signals or barrier semaphores. Data moves between devices by JAX's collectives and lax.ppermute only.
A program may use at most 64 MiB of HBM per device.

```python
import jax
import jax.numpy as jnp
from jax import lax

N = 16384
NB = 256
REFL = 512


def draw_matrix(key, part):
    key = jax.random.fold_in(key, 11)
    values = jnp.clip(jax.random.normal(key, (N, N), jnp.float32), -6.0, 6.0)
    return (values + values.T) * 0.70710678


def draw_reflectors(key, part):
    key = jax.random.fold_in(key, 23)
    key_vals, key_rows, key_cols = jax.random.split(key, 3)
    values = jnp.clip(jax.random.normal(key_vals, (N, REFL), jnp.float32), -6.0, 6.0)
    low_row = -1.2
    row_scale = jnp.exp(jax.random.uniform(key_rows, (N,), jnp.float32, low_row, 1.1))
    col_scale = jnp.exp(jax.random.uniform(key_cols, (REFL,), jnp.float32, -0.69, 1.38))
    return values * row_scale[:, None] * col_scale[None, :] / jnp.sqrt(jnp.float32(N))


def setup_inputs(seed: int = 0) -> dict:
    seeds = jax.random.split(jax.random.key(seed), 3)
    return {
        "matrix": draw_matrix(jax.random.fold_in(seeds[2], 71), 0),
        "reflectors": draw_reflectors(jax.random.fold_in(seeds[2], 71), 0),
    }


def precise(left, right):
    return jnp.dot(left, right, precision=lax.Precision.HIGHEST, preferred_element_type=jnp.float32)


def invert_upper(gram_matrix):
    order = gram_matrix.shape[0]
    half_diag = 0.5 * jnp.diagonal(gram_matrix)
    strict = jnp.triu(gram_matrix, 1) / half_diag[:, None]
    identity = jnp.eye(order, dtype=jnp.float32)
    power = -strict
    result = identity + power
    reach = 2
    while reach < order:
        power = precise(power, power)
        result = precise(result, identity + power)
        reach = reach * 2
    return result / half_diag[None, :]


def reference(matrix, reflectors):
    index_rows = lax.broadcasted_iota(jnp.int32, (N, REFL), 0)
    pivot_row = lax.broadcasted_iota(jnp.int32, (N, REFL), 1) + NB
    vectors = jnp.where(index_rows < pivot_row, jnp.float32(0.0), jnp.where(index_rows == pivot_row, jnp.float32(1.0), reflectors))
    gram_matrix = precise(vectors.T, vectors)
    triangle = invert_upper(gram_matrix)
    products = precise(matrix, vectors)
    applied = precise(products, triangle)
    middle = precise(triangle.T, precise(vectors.T, applied))
    correction = applied - 0.5 * precise(vectors, middle)
    left_side = jnp.concatenate([vectors, correction], 1)
    right_side = jnp.concatenate([correction, vectors], 1)
    return matrix - precise(left_side, right_side.T)
```

```python
import jax
import jax.numpy as jnp
import numpy as np
from jax import lax
from jax.experimental import pallas as pl
from jax.experimental.pallas import tpu as pltpu
from jax.sharding import Mesh, PartitionSpec as P

NB = 256
BLOCK = 128
Y = 4
Z = 8
X = 4
CORES = 2
COLS = X * CORES
EVERY = ("y", "z", "x", "core")
ROW = ("y", "z")
COL = ("x", "core")


def product(left, right, contract, precision=lax.Precision.HIGHEST):
    return lax.dot_general(
        left, right, (((contract[0],), (contract[1],)), ((), ())),
        precision=precision, preferred_element_type=jnp.float32,
    )


def precise(left, right):
    return jnp.matmul(left, right, precision=lax.Precision.HIGHEST, preferred_element_type=jnp.float32)


def join_upper(inverse, strict, size):
    pairs = inverse.shape[0] // 2
    off = jnp.stack(
        [strict[(2 * i) * size : (2 * i + 1) * size, (2 * i + 1) * size : (2 * i + 2) * size] for i in range(pairs)]
    )
    first, second = inverse[0::2], inverse[1::2]
    corner = -precise(precise(first, off), second)
    top = jnp.concatenate([first, corner], 2)
    bottom = jnp.concatenate([jnp.zeros_like(corner), second], 2)
    return jnp.concatenate([top, bottom], 1)


def invert_upper(gram_matrix):
    order = gram_matrix.shape[0]
    rows = lax.broadcasted_iota(jnp.int32, (order, order), 0)
    cols = lax.broadcasted_iota(jnp.int32, (order, order), 1)
    diagonal = jnp.where(rows == cols, 0.5 * gram_matrix, 0.0)
    strict = jnp.where(rows < cols, gram_matrix, 0.0) / jnp.sum(diagonal, 1, keepdims=True)
    count = order // BLOCK
    power = -jnp.stack([strict[i * BLOCK : (i + 1) * BLOCK, i * BLOCK : (i + 1) * BLOCK] for i in range(count)])
    identity = jnp.eye(BLOCK, dtype=jnp.float32)[None]
    result = identity + power
    reach = 2
    while reach < BLOCK:
        power = precise(power, power)
        result = precise(result, identity + power)
        reach = reach * 2
    size = BLOCK
    while size < order:
        result = join_upper(result, strict, size)
        size = size * 2
    return result[0] / jnp.sum(diagonal, 0, keepdims=True)


def split(value):
    high = value.astype(jnp.bfloat16)
    return high, (value - high.astype(jnp.float32)).astype(jnp.bfloat16)


def three_pass(left, right, contract):
    dims = (((contract[0],), (contract[1],)), ((), ()))
    dot = lambda a, b: lax.dot_general(a, b, dims, preferred_element_type=jnp.float32)
    return dot(left[0], right[0]) + (dot(left[0], right[1]) + dot(left[1], right[0]))


def accumulate_kernel(left_ref, right_ref, out_ref):
    term = three_pass(split(left_ref[...]), split(right_ref[...]), (1, 0))

    @pl.when(pl.program_id(0) == 0)
    def _():
        out_ref[...] = term

    @pl.when(pl.program_id(0) > 0)
    def _():
        out_ref[...] += term


def long_product(left, right, depth=512):
    rows, steps = left.shape[0], left.shape[1] // depth
    columns = right.shape[1]
    return pl.pallas_call(
        accumulate_kernel,
        grid=(steps,),
        in_specs=[
            pl.BlockSpec((rows, depth), lambda k: (0, k)),
            pl.BlockSpec((depth, columns), lambda k: (k, 0)),
        ],
        out_specs=pl.BlockSpec((rows, columns), lambda k: (0, 0)),
        out_shape=jax.ShapeDtypeStruct((rows, columns), jnp.float32),
        compiler_params=pltpu.CompilerParams(vmem_limit_bytes=40 * 2**20),
        cost_estimate=pl.CostEstimate(
            flops=6 * rows * left.shape[1] * columns, bytes_accessed=4 * (left.size + right.size), transcendentals=0
        ),
    )(left, right)


def subtract_kernel(base_ref, left_ref, right_ref, out_ref, high_ref, low_ref):
    @pl.when(pl.program_id(0) == 0)
    def _():
        high_ref[...], low_ref[...] = split(left_ref[...])

    term = three_pass((high_ref[...], low_ref[...]), split(right_ref[...]), (1, 1))
    out_ref[...] = base_ref[...] - term


def subtract_product(base, left, right, width=256):
    rows, columns = base.shape
    depth = left.shape[1]
    return pl.pallas_call(
        subtract_kernel,
        grid=(columns // width,),
        in_specs=[
            pl.BlockSpec((rows, width), lambda j: (0, j)),
            pl.BlockSpec((rows, depth), lambda j: (0, 0)),
            pl.BlockSpec((width, depth), lambda j: (j, 0)),
        ],
        out_specs=pl.BlockSpec((rows, width), lambda j: (0, j)),
        out_shape=jax.ShapeDtypeStruct((rows, columns), jnp.float32),
        scratch_shapes=[pltpu.VMEM((rows, depth), jnp.bfloat16)] * 2,
        compiler_params=pltpu.CompilerParams(vmem_limit_bytes=40 * 2**20),
        cost_estimate=pl.CostEstimate(
            flops=6 * rows * columns * depth, bytes_accessed=4 * (2 * base.size + right.size), transcendentals=0
        ),
    )(base, left, right)


def exchange(value, axis):
    return lax.all_to_all(value, axis, 0, 0, tiled=True)


def spread(value, axis):
    return exchange(jnp.tile(value, (lax.axis_size(axis),) + (1,) * (value.ndim - 1)), axis)


def sum_pieces(value, count):
    return jnp.sum(value.reshape((count, value.shape[0] // count) + value.shape[1:]), 0)


def all_sum(value, axis):
    count = lax.axis_size(axis)
    piece = sum_pieces(exchange(value.reshape(count * 8, -1), axis), count)
    return spread(piece, axis).reshape(value.shape)


def after(value, other):
    return lax.optimization_barrier((value, other))[0]


TO_COLUMN = [
    (row * COLS + col, ((row % Y) * Z + col) * COLS + row // Y) for row in range(Y * Z) for col in range(COLS)
]


def per_device(matrix, reflectors):
    rows_block, reflector_count = reflectors.shape
    r, c = lax.axis_index(ROW), lax.axis_index(COL)
    index_rows = r * rows_block + lax.broadcasted_iota(jnp.int32, (rows_block, reflector_count), 0)
    pivot_row = lax.broadcasted_iota(jnp.int32, (rows_block, reflector_count), 1) + NB
    vec_rows = jnp.where(
        index_rows < pivot_row,
        jnp.float32(0.0),
        jnp.where(index_rows == pivot_row, jnp.float32(1.0), reflectors),
    )
    piece = rows_block // COLS
    vec_mine = lax.ppermute(lax.dynamic_slice_in_dim(vec_rows, c * piece, piece, 0), EVERY, TO_COLUMN)
    vec_cols = lax.all_gather(vec_mine, ROW, tiled=True)

    width = reflector_count // COLS
    vec_slice = lax.dynamic_slice_in_dim(vec_rows, c * width, width, 1)
    gram_slice = all_sum(after(product(vec_slice, vec_rows, (0, 0)), vec_mine), ROW)
    triangle = invert_upper(spread(gram_slice, COL))
    left_vec = product(vec_rows, triangle, (1, 1))

    vec_cols = after(vec_cols, left_vec)
    part = long_product(matrix, vec_cols)
    prod_piece = sum_pieces(exchange(part, COL), COLS)
    prod_mine = lax.ppermute(prod_piece, EVERY, TO_COLUMN)
    prod_cols = lax.all_gather(prod_mine, ROW, tiled=True)

    prod_rows = spread(after(prod_piece, prod_mine), COL)
    crossed = spread(all_sum(product(vec_slice, prod_rows, (0, 0), lax.Precision.HIGH), ROW), COL)
    crossed = 0.5 * (crossed + crossed.T)
    left_prod = prod_rows - product(left_vec, crossed, (1, 0), lax.Precision.HIGH)
    left_prod = product(left_prod, triangle, (1, 0), lax.Precision.HIGH)
    base = matrix - product(left_prod, vec_cols, (1, 1), lax.Precision.HIGH)
    return subtract_product(base, left_vec, prod_cols)


def solution(mesh):
    torus = Mesh(np.asarray(mesh.devices).reshape(Y, Z, X, CORES), EVERY)
    in_specs = (P(ROW, COL), P(ROW, None))
    out_specs = P(ROW, COL)
    return jax.shard_map(
        per_device, mesh=torus, in_specs=in_specs, out_specs=out_specs, check_vma=False
    )
```
